32 devices in a mesh: groups: 2 (over y), mem: 4 (over z), head: 2 (over x), pair: 2 (over core).
Axes of the slice: x: 2, y: 2, z: 4, core: 2. Of those that a mesh axis runs over, the one named last changes fastest.
Arguments:
- queries: bfloat16 [384, 4096], P(('groups', 'mem', 'pair'), 'head'), parts along dimension 0, may hold values from -17 to 17
- row_question: int32 [384], P(('groups', 'mem', 'pair')), parts along dimension 0, may hold values from 0 to 3
- keys: bfloat16 [8192, 4096], P(('groups', 'mem'), 'head'), parts along dimension 0, may hold values from -6 to 6
- values: bfloat16 [8192, 4096], P(('groups', 'mem'), 'head'), parts along dimension 0, may hold values from -6 to 6
- lengths: int32 [16], P(('groups', 'mem')), parts along dimension 0, may hold values from 64 to 512
- passage_question: int32 [16], P(('groups', 'mem')), parts along dimension 0, may hold values from 0 to 3, as said below
Outputs:
- attended: bfloat16 [384, 4096], P(('groups', 'mem', 'pair'), 'head'), parts along dimension 0
The draws below stay inside these ranges and needn't reach their ends.
There are 2 independent parts, one for each index of `groups`. The reference program is written for one: setup_inputs(seed, part) draws one part's arguments, and reference() takes and returns one part's arrays. A program takes and returns all parts, laid end to end along the dimension named above; each array names one. Nothing has to cross between parts.
Inputs may be any that keep to these rules, and one draw needn't show every extreme that they name: `passage_question`: every question of 0 to 3 owns at least one passage.
All inputs are finite; a program needn't handle non-finite values.
Results may differ from the reference program's by a relative error of at most 0.013.
Values may be sent and summed in bfloat16 or wider, within the bound.
A program may use at most 64 MiB of HBM per device.

```python
import jax
import jax.numpy as jnp
from jax import lax

H = 64
DH = 64
PLEN = 512
BATCH = 4
PASSAGES = 8
TOKENS = 4096
QROWS = 192


def key_base(key):
    return 0.35 * jax.random.truncated_normal(jax.random.fold_in(key, 11), -4.0, 4.0, (TOKENS, H * DH), jnp.float32)


def quest_rows(key):
    return jax.random.randint(jax.random.fold_in(key, 21), (QROWS,), 0, BATCH, dtype=jnp.int32)


def quest_passages(key):
    owners = jax.random.randint(jax.random.fold_in(key, 22), (PASSAGES,), 0, BATCH, dtype=jnp.int32)
    chosen = jax.random.permutation(jax.random.fold_in(key, 23), PASSAGES)[:BATCH]
    return owners.at[chosen].set(jnp.arange(BATCH, dtype=jnp.int32))


def draw_queries(key, part):
    key = jax.random.fold_in(key, 2)
    field = 0.35 * jax.random.truncated_normal(key, -4.0, 4.0, (QROWS, H * DH), jnp.float32)
    return field.astype(jnp.bfloat16)


def draw_keys(key, part):
    base = key_base(key)
    return base.astype(jnp.bfloat16)


def draw_row_question(key, part):
    return quest_rows(key)


def draw_passage_question(key, part):
    return quest_passages(key)


def draw_lengths(key, part):
    key = jax.random.fold_in(key, 3)
    counts = jax.random.randint(key, (PASSAGES,), PLEN // 8, PLEN + 1, dtype=jnp.int32)
    order = jax.random.permutation(jax.random.fold_in(key, 4), PASSAGES)
    return counts.at[order[0]].set(PLEN).at[order[1]].set(PLEN // 8)


def block_levels(stream_key, shape, shards, least, high):
    def one(axis_at, shards_of):
        draws = jax.random.uniform(jax.random.fold_in(jax.random.fold_in(stream_key, 6), axis_at), (shards_of,), jnp.float32, least / len(shards), high / len(shards))
        return jnp.repeat(jnp.exp(draws), shape[axis_at] // shards_of).reshape((-1,) + (1,) * (len(shape) - axis_at - 1))

    factor_of = one(*shards[0])
    for cut in shards[1:]:
        factor_of = factor_of * one(*cut)
    return factor_of


def normal_values(stream_key, shape, deviation, bound, pieces=(), kind=jnp.bfloat16):
    entries = jax.random.normal(stream_key, shape, jnp.float32) * deviation
    if len(pieces) > 0:
        entries = block_levels(stream_key, shape, pieces, -0.22, 0.18) * entries
    return jnp.clip(entries, min=-bound, max=bound).astype(kind)


def setup_inputs(seed: int = 0, part: int = 0) -> dict:
    seeds = jax.random.split(jax.random.key(seed), 7)
    part_keys = jax.random.split(jax.random.fold_in(seeds[6], part), 7)
    queries = draw_queries(jax.random.fold_in(jax.random.fold_in(seeds[6], part), 71), part)
    row_question = draw_row_question(jax.random.fold_in(jax.random.fold_in(seeds[6], part), 71), part)
    keys = draw_keys(jax.random.fold_in(jax.random.fold_in(seeds[6], part), 71), part)
    values = normal_values(part_keys[3], (TOKENS, H * DH), 1.0, 6.0, ((0, 4), (1, 2)))
    lengths = draw_lengths(jax.random.fold_in(jax.random.fold_in(seeds[6], part), 71), part)
    passage_question = draw_passage_question(jax.random.fold_in(jax.random.fold_in(seeds[6], part), 71), part)
    return dict(queries=queries, row_question=row_question, keys=keys, values=values, lengths=lengths, passage_question=passage_question)


NEG = -1.0e30


def reference(queries, row_question, keys, values, lengths, passage_question):
    positions = jnp.arange(PLEN, dtype=jnp.int32)
    tok_live = (positions[None, :] < lengths[:, None]).reshape(-1)
    tok_quest = jnp.broadcast_to(passage_question[:, None], (PASSAGES, PLEN)).reshape(-1)
    usable = (row_question[:, None] == tok_quest[None, :]) & tok_live[None, :]
    query_heads = queries.reshape(QROWS, H, DH).transpose(1, 0, 2)
    key_heads = keys.reshape(TOKENS, H, DH).transpose(1, 0, 2)
    value_heads = values.reshape(TOKENS, H, DH).transpose(1, 0, 2)

    def one_head(operands):
        query_part, key_part, value_part = operands
        scores = jnp.dot(query_part, key_part.T, preferred_element_type=jnp.float32)
        scores = jnp.where(usable, scores, NEG)
        maxima = jnp.max(scores, axis=1, keepdims=True)
        weights = jnp.where(usable, jnp.exp(scores - maxima), 0.0)
        totals = jnp.sum(weights, axis=1, keepdims=True)
        mixture = jnp.dot(weights.astype(jnp.bfloat16), value_part, preferred_element_type=jnp.float32)
        return mixture / totals

    outputs = lax.map(one_head, (query_heads, key_heads, value_heads))
    return outputs.transpose(1, 0, 2).reshape(QROWS, H * DH).astype(jnp.bfloat16)
```

```python
import functools

import jax
import jax.numpy as jnp
from jax import lax
from jax.experimental import pallas as pl
from jax.experimental.pallas import tpu as pltpu
from jax.sharding import PartitionSpec as P

DH = 64
LANES = 256
PACK = LANES // DH
TOP = 16
NEG = -1e30
MESH = pl.DeviceIdType.MESH


def kernel(
    n, rows, groups, slots,
    q_ref, quest_ref, k_hbm, v_hbm, len_ref, pq_ref, out_ref,
    qbuf, obuf, rbuf, stat, rstat, bias, onehot, kbuf, vbuf,
    k_sem, v_sem, qs_sem, qr_sem, os_sem, or_sem, ss_sem, sr_sem,
):
    me = lax.axis_index("mem")
    chunks = groups // 2
    both = 2 * rows
    block = min(n, 4)
    tokens = kbuf.shape[0]
    width = 2 * LANES

    def load(c, hbm, buf, sem):
        cols = pl.ds(pl.multiple_of(c * width, width), width)
        return pltpu.make_async_copy(hbm.at[:, cols], buf.at[:, cols], sem.at[c])

    for c in range(chunks):
        load(c, k_hbm, kbuf, k_sem).start()
        load(c, v_hbm, vbuf, v_sem).start()

    barrier = pltpu.get_barrier_semaphore()
    for k in range(1, n):
        pl.semaphore_signal(barrier, inc=1, device_id={"mem": lax.rem(me + k, n)}, device_id_type=MESH)

    onehot[...] = jnp.zeros_like(onehot)
    ids = lax.broadcasted_iota(jnp.int32, (TOP, rows), 0)
    onehot[:, :rows] = jnp.where(ids == quest_ref[...], 1.0, 0.0)
    qbuf[me, 0:TOP, :] = onehot[...].astype(jnp.bfloat16)
    for c in range(chunks):
        halves = [
            q_ref[:, (2 * c + g) * LANES : (2 * c + g + 1) * LANES].astype(jnp.float32) for g in range(2)
        ]
        qbuf[me, TOP + both * c : TOP + both * (c + 1), :] = jnp.concatenate(halves, 0).astype(jnp.bfloat16)

    pl.semaphore_wait(barrier, n - 1)

    def query_copy(k, c, slot):
        span = pl.ds(0, TOP + both) if c == 0 else pl.ds(TOP + both * c, both)
        return pltpu.make_async_remote_copy(
            src_ref=qbuf.at[slot, span],
            dst_ref=qbuf.at[slot, span],
            send_sem=qs_sem.at[k, c],
            recv_sem=qr_sem.at[k, c],
            device_id={"mem": lax.rem(me + k, n)},
            device_id_type=MESH,
        )

    def result_copy(k, c, there, here):
        span = pl.ds(pl.multiple_of(both * c, 16), both)
        return pltpu.make_async_remote_copy(
            src_ref=obuf.at[there, span],
            dst_ref=rbuf.at[here, span],
            send_sem=os_sem.at[k, c],
            recv_sem=or_sem.at[k, c],
            device_id={"mem": lax.rem(me + k, n)},
            device_id_type=MESH,
        )

    def stat_copy(k, there, here):
        return pltpu.make_async_remote_copy(
            src_ref=stat.at[there],
            dst_ref=rstat.at[here],
            send_sem=ss_sem.at[k],
            recv_sem=sr_sem.at[k],
            device_id={"mem": lax.rem(me + k, n)},
            device_id_type=MESH,
        )

    for c in range(chunks):
        for k in range(1, n):
            query_copy(k, c, me).start()

    quest = lax.broadcasted_iota(jnp.int32, (TOP, tokens), 0)
    slot = lax.broadcasted_iota(jnp.int32, (TOP, tokens), 1)
    table = jnp.full((TOP, tokens), NEG, jnp.float32)
    for p in range(tokens // slots):
        good = (slot >= p * slots) & (slot < p * slots + len_ref[p]) & (quest == pq_ref[p])
        table = jnp.where(good, 0.0, table)
    table = table.astype(jnp.bfloat16)
    stat[...] = jnp.zeros_like(stat)

    lane_head = lax.broadcasted_iota(jnp.int32, (1, LANES), 1) // DH
    lane = lax.broadcasted_iota(jnp.int32, (1, 128), 1)

    for c in range(chunks):
        load(c, k_hbm, kbuf, k_sem).wait()
        load(c, v_hbm, vbuf, v_sem).wait()
        for k in range(1, n):
            query_copy(k, c, lax.rem(me + n - k, n)).wait_recv()

        def some(b, _, c=c):
            if c == 0:
                seen = [
                    jnp.transpose(qbuf[b * block + s, 0:TOP, 0:128].astype(jnp.float32))[:rows]
                    for s in range(block)
                ]
                bias[b] = jnp.dot(
                    jnp.concatenate(seen, 0).astype(jnp.bfloat16), table, preferred_element_type=jnp.float32
                )
            pair = [
                qbuf[b * block + s, TOP + both * c : TOP + both * (c + 1), :].astype(jnp.float32)
                for s in range(block)
            ]
            made = []
            found = [stat[b * block + s] for s in range(block)]
            for g in range(2):
                cols = slice((2 * c + g) * LANES, (2 * c + g + 1) * LANES)
                q4 = jnp.concatenate([x[g * rows : (g + 1) * rows] for x in pair], 0)
                spread = jnp.concatenate([jnp.where(lane_head == h, q4, 0.0) for h in range(PACK)], 0)
                scores = lax.dot_general(
                    spread.astype(jnp.bfloat16), kbuf[:, cols], (((1,), (1,)), ((), ())),
                    preferred_element_type=jnp.float32,
                )
                scores = scores.reshape(PACK, block * rows, tokens) + bias[b][None]
                maxima = jnp.max(scores, axis=2, keepdims=True)
                weights = jnp.exp(scores - maxima)
                totals = jnp.sum(weights, axis=2, keepdims=True)
                mixture = jnp.dot(
                    weights.astype(jnp.bfloat16).reshape(PACK * block * rows, tokens), vbuf[:, cols],
                    preferred_element_type=jnp.float32,
                ).reshape(PACK, block * rows, LANES)
                mixture = mixture / totals
                picked = mixture[0]
                for h in range(1, PACK):
                    picked = jnp.where(lane_head == h, mixture[h], picked)
                made.append(picked)
                for h in range(PACK):
                    at = (2 * c + g) * PACK + h
                    for s in range(block):
                        part = slice(s * rows, (s + 1) * rows)
                        found[s] = jnp.where(lane == at, maxima[h, part], found[s])
                        found[s] = jnp.where(lane == 64 + at, totals[h, part], found[s])
            for s in range(block):
                part = slice(s * rows, (s + 1) * rows)
                stat[b * block + s] = found[s]
                obuf[b * block + s, both * c : both * (c + 1), :] = jnp.concatenate(
                    [made[0][part], made[1][part]], 0
                ).astype(jnp.bfloat16)
            return 0

        if n == block:
            some(0, 0)
        else:
            lax.fori_loop(0, n // block, some, 0)
        if c == chunks - 1:
            for k in range(1, n):
                stat_copy(k, lax.rem(me + k, n), me).start()
        for k in range(1, n):
            result_copy(k, c, lax.rem(me + k, n), me).start()

    rstat[me] = stat[me]
    for c in range(chunks):
        span = slice(both * c, both * (c + 1))
        rbuf[me, span, :] = obuf[me, span, :]

    for k in range(1, n):
        stat_copy(k, me, lax.rem(me + n - k, n)).wait_recv()
    top = rstat[0]
    for s in range(1, n):
        top = jnp.maximum(top, rstat[s])
    shares = []
    for s in range(n):
        now = rstat[s]
        shares.append(jnp.exp(now - top) * pltpu.roll(now, 64, 1))
    whole = functools.reduce(lambda a, b: a + b, shares)
    shares = [jnp.where(lane < groups * PACK, x / whole, 0.0) for x in shares]
    shares = jnp.concatenate(shares, 0)
    high = shares.astype(jnp.bfloat16)
    low = (shares - high.astype(jnp.float32)).astype(jnp.bfloat16)
    at_head = lax.broadcasted_iota(jnp.int32, (128, LANES), 0)
    at_lane = lax.broadcasted_iota(jnp.int32, (128, LANES), 1) // DH
    for c in range(chunks):
        for k in range(1, n):
            result_copy(k, c, me, lax.rem(me + n - k, n)).wait_recv()
        factor = []
        for g in range(2):
            expand = jnp.where(at_head == (2 * c + g) * PACK + at_lane, 1.0, 0.0).astype(jnp.bfloat16)
            factor.append(
                jnp.dot(high, expand, preferred_element_type=jnp.float32)
                + jnp.dot(low, expand, preferred_element_type=jnp.float32)
            )
        sums = [0.0, 0.0]
        for s in range(n):
            got = rbuf[s, both * c : both * (c + 1), :].astype(jnp.float32)
            for g in range(2):
                sums[g] = sums[g] + got[g * rows : (g + 1) * rows] * factor[g][s * rows : (s + 1) * rows]
        for g in range(2):
            out_ref[:, (2 * c + g) * LANES : (2 * c + g + 1) * LANES] = sums[g].astype(jnp.bfloat16)

    for k in range(1, n):
        for c in range(chunks):
            query_copy(k, c, me).wait_send()
            result_copy(k, c, lax.rem(me + k, n), me).wait_send()
        stat_copy(k, lax.rem(me + k, n), me).wait_send()


def body(n, queries, row_question, keys, values, lengths, passage_question):
    rows, width = queries.shape
    tokens = keys.shape[0]
    groups = width // LANES
    chunks = groups // 2
    block = min(n, 4)
    bf16, f32 = jnp.bfloat16, jnp.float32
    vmem = pl.BlockSpec(memory_space=pltpu.VMEM)
    smem = pl.BlockSpec(memory_space=pltpu.SMEM)
    anywhere = pl.BlockSpec(memory_space=pl.ANY)
    return pl.pallas_call(
        functools.partial(kernel, n, rows, groups, tokens // lengths.shape[0]),
        out_shape=jax.ShapeDtypeStruct((rows, width), bf16),
        in_specs=[vmem, vmem, anywhere, anywhere, smem, smem],
        out_specs=vmem,
        scratch_shapes=[
            pltpu.VMEM((n, TOP + groups * rows, LANES), bf16),
            pltpu.VMEM((n, groups * rows, LANES), bf16),
            pltpu.VMEM((n, groups * rows, LANES), bf16),
            pltpu.VMEM((n, rows, 128), f32),
            pltpu.VMEM((n, rows, 128), f32),
            pltpu.VMEM((n // block, block * rows, tokens), f32),
            pltpu.VMEM((TOP, LANES), f32),
            pltpu.VMEM((tokens, width), bf16),
            pltpu.VMEM((tokens, width), bf16),
            pltpu.SemaphoreType.DMA((chunks,)),
            pltpu.SemaphoreType.DMA((chunks,)),
            pltpu.SemaphoreType.DMA((n, chunks)),
            pltpu.SemaphoreType.DMA((n, chunks)),
            pltpu.SemaphoreType.DMA((n, chunks)),
            pltpu.SemaphoreType.DMA((n, chunks)),
            pltpu.SemaphoreType.DMA((n,)),
            pltpu.SemaphoreType.DMA((n,)),
        ],
        compiler_params=pltpu.CompilerParams(
            collective_id=0, has_side_effects=True, vmem_limit_bytes=44 * 1024 * 1024
        ),
        cost_estimate=pl.CostEstimate(
            flops=4 * n * rows * width * tokens,
            bytes_accessed=4 * tokens * width,
            transcendentals=n * rows * tokens * (width // DH),
        ),
    )(queries, row_question.reshape(1, rows), keys, values, lengths, passage_question)


def solution(mesh):
    in_specs = (
        P(("groups", "mem", "pair"), "head"),
        P(("groups", "mem", "pair")),
        P(("groups", "mem"), "head"),
        P(("groups", "mem"), "head"),
        P(("groups", "mem")),
        P(("groups", "mem")),
    )
    out_specs = P(("groups", "mem", "pair"), "head")
    return jax.shard_map(
        functools.partial(body, mesh.shape["mem"]), mesh=mesh, in_specs=in_specs, out_specs=out_specs,
        check_vma=False,
    )
```

```python
import functools

import jax
import jax.numpy as jnp
from jax import lax
from jax.experimental import pallas as pl
from jax.experimental.pallas import tpu as pltpu
from jax.sharding import PartitionSpec as P

DH = 64
LANES = 256
PACK = LANES // DH
TOP = 16
NEG = -1e30
MESH = pl.DeviceIdType.MESH


def kernel(
    n, rows, groups, slots,
    q_ref, quest_ref, k_hbm, v_hbm, len_ref, pq_ref, out_ref,
    qbuf, obuf, rbuf, stat, rstat, bias, onehot, kbuf, vbuf,
    k_sem, v_sem, qs_sem, qr_sem, os_sem, or_sem, ss_sem, sr_sem,
):
    me = lax.axis_index("mem")
    chunks = groups // 2
    both = 2 * rows
    block = min(n, 4)
    tokens = kbuf.shape[0]
    width = 2 * LANES

    def load(c, hbm, buf, sem):
        cols = pl.ds(pl.multiple_of(c * width, width), width)
        return pltpu.make_async_copy(hbm.at[:, cols], buf.at[:, cols], sem.at[c])

    for c in range(chunks):
        load(c, k_hbm, kbuf, k_sem).start()
        load(c, v_hbm, vbuf, v_sem).start()

    barrier = pltpu.get_barrier_semaphore()
    for k in range(1, n):
        pl.semaphore_signal(barrier, inc=1, device_id={"mem": lax.rem(me + k, n)}, device_id_type=MESH)

    onehot[...] = jnp.zeros_like(onehot)
    ids = lax.broadcasted_iota(jnp.int32, (TOP, rows), 0)
    onehot[:, :rows] = jnp.where(ids == quest_ref[...], 1.0, 0.0)
    qbuf[me, 0:TOP, :] = onehot[...].astype(jnp.bfloat16)
    for c in range(chunks):
        halves = [
            q_ref[:, (2 * c + g) * LANES : (2 * c + g + 1) * LANES].astype(jnp.float32) for g in range(2)
        ]
        qbuf[me, TOP + both * c : TOP + both * (c + 1), :] = jnp.concatenate(halves, 0).astype(jnp.bfloat16)

    pl.semaphore_wait(barrier, n - 1)

    def query_copy(k, c, slot):
        span = pl.ds(0, TOP + both) if c == 0 else pl.ds(TOP + both * c, both)
        return pltpu.make_async_remote_copy(
            src_ref=qbuf.at[slot, span],
            dst_ref=qbuf.at[slot, span],
            send_sem=qs_sem.at[k, c],
            recv_sem=qr_sem.at[k, c],
            device_id={"mem": lax.rem(me + k, n)},
            device_id_type=MESH,
        )

    def result_copy(k, c, there, here):
        span = pl.ds(pl.multiple_of(both * c, 16), both)
        return pltpu.make_async_remote_copy(
            src_ref=obuf.at[there, span],
            dst_ref=rbuf.at[here, span],
            send_sem=os_sem.at[k, c],
            recv_sem=or_sem.at[k, c],
            device_id={"mem": lax.rem(me + k, n)},
            device_id_type=MESH,
        )

    def stat_copy(k, there, here):
        return pltpu.make_async_remote_copy(
            src_ref=stat.at[there],
            dst_ref=rstat.at[here],
            send_sem=ss_sem.at[k],
            recv_sem=sr_sem.at[k],
            device_id={"mem": lax.rem(me + k, n)},
            device_id_type=MESH,
        )

    for c in range(chunks):
        for k in range(1, n):
            query_copy(k, c, me).start()

    quest = lax.broadcasted_iota(jnp.int32, (TOP, tokens), 0)
    slot = lax.broadcasted_iota(jnp.int32, (TOP, tokens), 1)
    table = jnp.full((TOP, tokens), NEG, jnp.float32)
    for p in range(tokens // slots):
        good = (slot >= p * slots) & (slot < p * slots + len_ref[p]) & (quest == pq_ref[p])
        table = jnp.where(good, 0.0, table)
    table = table.astype(jnp.bfloat16)
    stat[...] = jnp.zeros_like(stat)

    lane_head = lax.broadcasted_iota(jnp.int32, (1, LANES), 1) // DH
    lane = lax.broadcasted_iota(jnp.int32, (1, 128), 1)

    for c in range(chunks):
        load(c, k_hbm, kbuf, k_sem).wait()
        load(c, v_hbm, vbuf, v_sem).wait()
        for k in range(1, n):
            query_copy(k, c, lax.rem(me + n - k, n)).wait_recv()

        def some(b, _, c=c):
            if c == 0:
                seen = [
                    jnp.transpose(qbuf[b * block + s, 0:TOP, 0:128].astype(jnp.float32))[:rows]
                    for s in range(block)
                ]
                bias[b] = jnp.dot(
                    jnp.concatenate(seen, 0).astype(jnp.bfloat16), table, preferred_element_type=jnp.float32
                )
            pair = [
                qbuf[b * block + s, TOP + both * c : TOP + both * (c + 1), :].astype(jnp.float32)
                for s in range(block)
            ]
            made = []
            found = [stat[b * block + s] for s in range(block)]
            for g in range(2):
                cols = slice((2 * c + g) * LANES, (2 * c + g + 1) * LANES)
                q4 = jnp.concatenate([x[g * rows : (g + 1) * rows] for x in pair], 0)
                spread = jnp.concatenate([jnp.where(lane_head == h, q4, 0.0) for h in range(PACK)], 0)
                scores = lax.dot_general(
                    spread.astype(jnp.bfloat16), kbuf[:, cols], (((1,), (1,)), ((), ())),
                    preferred_element_type=jnp.float32,
                )
                scores = scores.reshape(PACK, block * rows, tokens) + bias[b][None]
                maxima = jnp.max(scores, axis=2, keepdims=True)
                weights = jnp.exp(scores - maxima)
                totals = jnp.sum(weights, axis=2, keepdims=True)
                mixture = jnp.dot(
                    weights.astype(jnp.bfloat16).reshape(PACK * block * rows, tokens), vbuf[:, cols],
                    preferred_element_type=jnp.float32,
                ).reshape(PACK, block * rows, LANES)
                mixture = mixture / totals
                picked = mixture[0]
                for h in range(1, PACK):
                    picked = jnp.where(lane_head == h, mixture[h], picked)
                made.append(picked)
                for h in range(PACK):
                    at = (2 * c + g) * PACK + h
                    for s in range(block):
                        part = slice(s * rows, (s + 1) * rows)
                        found[s] = jnp.where(lane == at, maxima[h, part], found[s])
                        found[s] = jnp.where(lane == 64 + at, totals[h, part], found[s])
            for s in range(block):
                part = slice(s * rows, (s + 1) * rows)
                stat[b * block + s] = found[s]
                obuf[b * block + s, both * c : both * (c + 1), :] = jnp.concatenate(
                    [made[0][part], made[1][part]], 0
                ).astype(jnp.bfloat16)
            return 0

        if n == block:
            some(0, 0)
        else:
            lax.fori_loop(0, n // block, some, 0)
        if c == chunks - 1:
            for k in range(1, n):
                stat_copy(k, lax.rem(me + k, n), me).start()
        for k in range(1, n):
            result_copy(k, c, lax.rem(me + k, n), me).start()

    rstat[me] = stat[me]
    for c in range(chunks):
        span = slice(both * c, both * (c + 1))
        rbuf[me, span, :] = obuf[me, span, :]

    for k in range(1, n):
        stat_copy(k, me, lax.rem(me + n - k, n)).wait_recv()
    top = rstat[0]
    for s in range(1, n):
        top = jnp.maximum(top, rstat[s])
    shares = []
    for s in range(n):
        now = rstat[s]
        shares.append(jnp.exp(now - top) * pltpu.roll(now, 64, 1))
    whole = functools.reduce(lambda a, b: a + b, shares)
    shares = [jnp.where(lane < groups * PACK, x / whole, 0.0) for x in shares]
    shares = jnp.concatenate(shares, 0)
    high = shares.astype(jnp.bfloat16)
    low = (shares - high.astype(jnp.float32)).astype(jnp.bfloat16)
    at_head = lax.broadcasted_iota(jnp.int32, (128, LANES), 0)
    at_lane = lax.broadcasted_iota(jnp.int32, (128, LANES), 1) // DH
    for c in range(chunks):
        for k in range(1, n):
            result_copy(k, c, me, lax.rem(me + n - k, n)).wait_recv()
        factor = []
        for g in range(2):
            expand = jnp.where(at_head == (2 * c + g) * PACK + at_lane, 1.0, 0.0).astype(jnp.bfloat16)
            factor.append(
                jnp.dot(high, expand, preferred_element_type=jnp.float32)
                + jnp.dot(low, expand, preferred_element_type=jnp.float32)
            )
        sums = [0.0, 0.0]
        for s in range(n):
            got = rbuf[s, both * c : both * (c + 1), :].astype(jnp.float32)
            for g in range(2):
                sums[g] = sums[g] + got[g * rows : (g + 1) * rows] * factor[g][s * rows : (s + 1) * rows]
        for g in range(2):
            out_ref[:, (2 * c + g) * LANES : (2 * c + g + 1) * LANES] = sums[g].astype(jnp.bfloat16)

    for k in range(1, n):
        for c in range(chunks):
            query_copy(k, c, me).wait_send()
            result_copy(k, c, lax.rem(me + k, n), me).wait_send()
        stat_copy(k, lax.rem(me + k, n), me).wait_send()


def body(n, queries, row_question, keys, values, lengths, passage_question):
    rows, width = queries.shape
    tokens = keys.shape[0]
    groups = width // LANES
    chunks = groups // 2
    block = min(n, 4)
    bf16, f32 = jnp.bfloat16, jnp.float32
    vmem = pl.BlockSpec(memory_space=pltpu.VMEM)
    smem = pl.BlockSpec(memory_space=pltpu.SMEM)
    anywhere = pl.BlockSpec(memory_space=pl.ANY)
    return pl.pallas_call(
        functools.partial(kernel, n, rows, groups, tokens // lengths.shape[0]),
        out_shape=jax.ShapeDtypeStruct((rows, width), bf16),
        in_specs=[vmem, vmem, anywhere, anywhere, smem, smem],
        out_specs=vmem,
        scratch_shapes=[
            pltpu.VMEM((n, TOP + groups * rows, LANES), bf16),
            pltpu.VMEM((n, groups * rows, LANES), bf16),
            pltpu.VMEM((n, groups * rows, LANES), bf16),
            pltpu.VMEM((n, rows, 128), f32),
            pltpu.VMEM((n, rows, 128), f32),
            pltpu.VMEM((n // block, block * rows, tokens), f32),
            pltpu.VMEM((TOP, LANES), f32),
            pltpu.VMEM((tokens, width), bf16),
            pltpu.VMEM((tokens, width), bf16),
            pltpu.SemaphoreType.DMA((chunks,)),
            pltpu.SemaphoreType.DMA((chunks,)),
            pltpu.SemaphoreType.DMA((n, chunks)),
            pltpu.SemaphoreType.DMA((n, chunks)),
            pltpu.SemaphoreType.DMA((n, chunks)),
            pltpu.SemaphoreType.DMA((n, chunks)),
            pltpu.SemaphoreType.DMA((n,)),
            pltpu.SemaphoreType.DMA((n,)),
        ],
        compiler_params=pltpu.CompilerParams(
            collective_id=0, has_side_effects=True, vmem_limit_bytes=60 * 1024 * 1024
        ),
        cost_estimate=pl.CostEstimate(
            flops=4 * n * rows * width * tokens,
            bytes_accessed=4 * tokens * width,
            transcendentals=n * rows * tokens * (width // DH),
        ),
    )(queries, row_question.reshape(1, rows), keys, values, lengths, passage_question)


def solution(mesh):
    in_specs = (
        P(("groups", "mem", "pair"), "head"),
        P(("groups", "mem", "pair")),
        P(("groups", "mem"), "head"),
        P(("groups", "mem"), "head"),
        P(("groups", "mem")),
        P(("groups", "mem")),
    )
    out_specs = P(("groups", "mem", "pair"), "head")
    return jax.shard_map(
        functools.partial(body, mesh.shape["mem"]), mesh=mesh, in_specs=in_specs, out_specs=out_specs,
        check_vma=False,
    )
```

```python
import functools

import jax
import jax.numpy as jnp
from jax import lax
from jax.experimental import pallas as pl
from jax.experimental.pallas import tpu as pltpu
from jax.sharding import PartitionSpec as P

DH = 64
LANES = 256
PACK = LANES // DH
TOP = 16
NEG = -1e30
MESH = pl.DeviceIdType.MESH


def kernel(
    n, rows, groups, slots,
    q_ref, quest_ref, k_hbm, v_hbm, len_ref, pq_ref, out_ref,
    qbuf, obuf, rbuf, stat, rstat, bias, onehot, kbuf, vbuf,
    k_sem, v_sem, qs_sem, qr_sem, os_sem, or_sem, ss_sem, sr_sem,
):
    me = lax.axis_index("mem")
    chunks = groups // 2
    both = 2 * rows
    block = min(n, 4)
    tokens = kbuf.shape[0]
    width = 2 * LANES

    def load(c, hbm, buf, sem):
        cols = pl.ds(pl.multiple_of(c * width, width), width)
        return pltpu.make_async_copy(hbm.at[:, cols], buf.at[:, cols], sem.at[c])

    for c in range(chunks):
        load(c, k_hbm, kbuf, k_sem).start()
        load(c, v_hbm, vbuf, v_sem).start()

    barrier = pltpu.get_barrier_semaphore()
    for k in range(1, n):
        pl.semaphore_signal(barrier, inc=1, device_id={"mem": lax.rem(me + k, n)}, device_id_type=MESH)

    onehot[...] = jnp.zeros_like(onehot)
    ids = lax.broadcasted_iota(jnp.int32, (TOP, rows), 0)
    onehot[:, :rows] = jnp.where(ids == quest_ref[...], 1.0, 0.0)
    qbuf[me, 0:TOP, :] = onehot[...].astype(jnp.bfloat16)
    for c in range(chunks):
        halves = [
            q_ref[:, (2 * c + g) * LANES : (2 * c + g + 1) * LANES].astype(jnp.float32) for g in range(2)
        ]
        qbuf[me, TOP + both * c : TOP + both * (c + 1), :] = jnp.concatenate(halves, 0).astype(jnp.bfloat16)

    pl.semaphore_wait(barrier, n - 1)

    def query_copy(k, c, slot):
        span = pl.ds(0, TOP + both) if c == 0 else pl.ds(TOP + both * c, both)
        return pltpu.make_async_remote_copy(
            src_ref=qbuf.at[slot, span],
            dst_ref=qbuf.at[slot, span],
            send_sem=qs_sem.at[k, c],
            recv_sem=qr_sem.at[k, c],
            device_id={"mem": lax.rem(me + k, n)},
            device_id_type=MESH,
        )

    def relay(c):
        span = pl.ds(0, TOP + both) if c == 0 else pl.ds(TOP + both * c, both)
        place = qbuf.at[lax.rem(me + n - 2, n), span]
        return pltpu.make_async_remote_copy(
            src_ref=place,
            dst_ref=place,
            send_sem=qs_sem.at[0, c],
            recv_sem=qr_sem.at[lax.rem(2 * me - 1 + n, n), c],
            device_id={"mem": lax.rem(3 * (me - 1) + 3 * n, n)},
            device_id_type=MESH,
        )

    def pass_on(c):
        if n == 4:
            query_copy(2, c, lax.rem(me + n - 2, n)).wait_recv()

            @pl.when((me == 1) | (me == 2))
            def _():
                relay(c).start()

    def result_copy(k, c, there, here):
        span = pl.ds(pl.multiple_of(both * c, 16), both)
        return pltpu.make_async_remote_copy(
            src_ref=obuf.at[there, span],
            dst_ref=rbuf.at[here, span],
            send_sem=os_sem.at[k, c],
            recv_sem=or_sem.at[k, c],
            device_id={"mem": lax.rem(me + k, n)},
            device_id_type=MESH,
        )

    def stat_copy(k, there, here):
        return pltpu.make_async_remote_copy(
            src_ref=stat.at[there],
            dst_ref=rstat.at[here],
            send_sem=ss_sem.at[k],
            recv_sem=sr_sem.at[k],
            device_id={"mem": lax.rem(me + k, n)},
            device_id_type=MESH,
        )

    for c in range(chunks):
        for k in [n // 2] + [x for x in range(1, n) if x != n // 2]:
            if n == 4 and k != 2:

                @pl.when(jnp.abs(me - lax.rem(me + k, n)) != 3)
                def _(k=k, c=c):
                    query_copy(k, c, me).start()
            else:
                query_copy(k, c, me).start()

    quest = lax.broadcasted_iota(jnp.int32, (TOP, tokens), 0)
    slot = lax.broadcasted_iota(jnp.int32, (TOP, tokens), 1)
    table = jnp.full((TOP, tokens), NEG, jnp.float32)
    for p in range(tokens // slots):
        good = (slot >= p * slots) & (slot < p * slots + len_ref[p]) & (quest == pq_ref[p])
        table = jnp.where(good, 0.0, table)
    table = table.astype(jnp.bfloat16)
    stat[...] = jnp.zeros_like(stat)

    lane_head = lax.broadcasted_iota(jnp.int32, (1, LANES), 1) // DH
    lane = lax.broadcasted_iota(jnp.int32, (1, 128), 1)

    for c in range(chunks):
        load(c, k_hbm, kbuf, k_sem).wait()
        load(c, v_hbm, vbuf, v_sem).wait()
        if c == 0:
            pass_on(0)
        if c + 1 < chunks:
            pass_on(c + 1)
        for k in range(1, n):
            if n != 4 or k != 2:
                query_copy(k, c, lax.rem(me + n - k, n)).wait_recv()

        def some(b, _, c=c):
            if c == 0:
                seen = [
                    jnp.transpose(qbuf[b * block + s, 0:TOP, 0:128].astype(jnp.float32))[:rows]
                    for s in range(block)
                ]
                bias[b] = jnp.dot(
                    jnp.concatenate(seen, 0).astype(jnp.bfloat16), table, preferred_element_type=jnp.float32
                )
            pair = [
                qbuf[b * block + s, TOP + both * c : TOP + both * (c + 1), :].astype(jnp.float32)
                for s in range(block)
            ]
            made = []
            found = [stat[b * block + s] for s in range(block)]
            for g in range(2):
                cols = slice((2 * c + g) * LANES, (2 * c + g + 1) * LANES)
                q4 = jnp.concatenate([x[g * rows : (g + 1) * rows] for x in pair], 0)
                spread = jnp.concatenate([jnp.where(lane_head == h, q4, 0.0) for h in range(PACK)], 0)
                scores = lax.dot_general(
                    spread.astype(jnp.bfloat16), kbuf[:, cols], (((1,), (1,)), ((), ())),
                    preferred_element_type=jnp.float32,
                )
                scores = scores.reshape(PACK, block * rows, tokens) + bias[b][None]
                maxima = jnp.max(scores, axis=2, keepdims=True)
                weights = jnp.exp(scores - maxima)
                totals = jnp.sum(weights, axis=2, keepdims=True)
                mixture = jnp.dot(
                    weights.astype(jnp.bfloat16).reshape(PACK * block * rows, tokens), vbuf[:, cols],
                    preferred_element_type=jnp.float32,
                ).reshape(PACK, block * rows, LANES)
                mixture = mixture / totals
                picked = mixture[0]
                for h in range(1, PACK):
                    picked = jnp.where(lane_head == h, mixture[h], picked)
                made.append(picked)
                for h in range(PACK):
                    at = (2 * c + g) * PACK + h
                    for s in range(block):
                        part = slice(s * rows, (s + 1) * rows)
                        found[s] = jnp.where(lane == at, maxima[h, part], found[s])
                        found[s] = jnp.where(lane == 64 + at, totals[h, part], found[s])
            for s in range(block):
                part = slice(s * rows, (s + 1) * rows)
                stat[b * block + s] = found[s]
                obuf[b * block + s, both * c : both * (c + 1), :] = jnp.concatenate(
                    [made[0][part], made[1][part]], 0
                ).astype(jnp.bfloat16)
            return 0

        if n == block:
            some(0, 0)
        else:
            lax.fori_loop(0, n // block, some, 0)
        if c == chunks - 1:
            for k in range(1, n):
                stat_copy(k, lax.rem(me + k, n), me).start()
        for k in [n // 2] + [x for x in range(1, n) if x != n // 2]:
            result_copy(k, c, lax.rem(me + k, n), me).start()

    rstat[me] = stat[me]
    for c in range(chunks):
        span = slice(both * c, both * (c + 1))
        rbuf[me, span, :] = obuf[me, span, :]

    for k in range(1, n):
        stat_copy(k, me, lax.rem(me + n - k, n)).wait_recv()
    top = rstat[0]
    for s in range(1, n):
        top = jnp.maximum(top, rstat[s])
    shares = []
    for s in range(n):
        now = rstat[s]
        shares.append(jnp.exp(now - top) * pltpu.roll(now, 64, 1))
    whole = functools.reduce(lambda a, b: a + b, shares)
    shares = [jnp.where(lane < groups * PACK, x / whole, 0.0) for x in shares]
    shares = jnp.concatenate(shares, 0)
    high = shares.astype(jnp.bfloat16)
    low = (shares - high.astype(jnp.float32)).astype(jnp.bfloat16)
    at_head = lax.broadcasted_iota(jnp.int32, (128, LANES), 0)
    at_lane = lax.broadcasted_iota(jnp.int32, (128, LANES), 1) // DH
    for c in range(chunks):
        for k in range(1, n):
            result_copy(k, c, me, lax.rem(me + n - k, n)).wait_recv()
        factor = []
        for g in range(2):
            expand = jnp.where(at_head == (2 * c + g) * PACK + at_lane, 1.0, 0.0).astype(jnp.bfloat16)
            factor.append(
                jnp.dot(high, expand, preferred_element_type=jnp.float32)
                + jnp.dot(low, expand, preferred_element_type=jnp.float32)
            )
        sums = [0.0, 0.0]
        for s in range(n):
            got = rbuf[s, both * c : both * (c + 1), :].astype(jnp.float32)
            for g in range(2):
                sums[g] = sums[g] + got[g * rows : (g + 1) * rows] * factor[g][s * rows : (s + 1) * rows]
        for g in range(2):
            out_ref[:, (2 * c + g) * LANES : (2 * c + g + 1) * LANES] = sums[g].astype(jnp.bfloat16)

    for k in range(1, n):
        for c in range(chunks):
            if n == 4 and k != 2:

                @pl.when(jnp.abs(me - lax.rem(me + k, n)) != 3)
                def _(k=k, c=c):
                    query_copy(k, c, me).wait_send()

            else:
                query_copy(k, c, me).wait_send()
            if n == 4 and k == 2:

                @pl.when((me == 1) | (me == 2))
                def _(c=c):
                    relay(c).wait_send()

            result_copy(k, c, lax.rem(me + k, n), me).wait_send()
        stat_copy(k, lax.rem(me + k, n), me).wait_send()


def body(n, queries, row_question, keys, values, lengths, passage_question):
    rows, width = queries.shape
    tokens = keys.shape[0]
    groups = width // LANES
    chunks = groups // 2
    block = min(n, 4)
    bf16, f32 = jnp.bfloat16, jnp.float32
    vmem = pl.BlockSpec(memory_space=pltpu.VMEM)
    smem = pl.BlockSpec(memory_space=pltpu.SMEM)
    anywhere = pl.BlockSpec(memory_space=pl.ANY)
    return pl.pallas_call(
        functools.partial(kernel, n, rows, groups, tokens // lengths.shape[0]),
        out_shape=jax.ShapeDtypeStruct((rows, width), bf16),
        in_specs=[vmem, vmem, anywhere, anywhere, smem, smem],
        out_specs=vmem,
        scratch_shapes=[
            pltpu.VMEM((n, TOP + groups * rows, LANES), bf16),
            pltpu.VMEM((n, groups * rows, LANES), bf16),
            pltpu.VMEM((n, groups * rows, LANES), bf16),
            pltpu.VMEM((n, rows, 128), f32),
            pltpu.VMEM((n, rows, 128), f32),
            pltpu.VMEM((n // block, block * rows, tokens), f32),
            pltpu.VMEM((TOP, LANES), f32),
            pltpu.VMEM((tokens, width), bf16),
            pltpu.VMEM((tokens, width), bf16),
            pltpu.SemaphoreType.DMA((chunks,)),
            pltpu.SemaphoreType.DMA((chunks,)),
            pltpu.SemaphoreType.DMA((n, chunks)),
            pltpu.SemaphoreType.DMA((n, chunks)),
            pltpu.SemaphoreType.DMA((n, chunks)),
            pltpu.SemaphoreType.DMA((n, chunks)),
            pltpu.SemaphoreType.DMA((n,)),
            pltpu.SemaphoreType.DMA((n,)),
        ],
        compiler_params=pltpu.CompilerParams(
            collective_id=0, has_side_effects=True, vmem_limit_bytes=60 * 1024 * 1024
        ),
        cost_estimate=pl.CostEstimate(
            flops=4 * n * rows * width * tokens,
            bytes_accessed=4 * tokens * width,
            transcendentals=n * rows * tokens * (width // DH),
        ),
    )(queries, row_question.reshape(1, rows), keys, values, lengths, passage_question)


def solution(mesh):
    in_specs = (
        P(("groups", "mem", "pair"), "head"),
        P(("groups", "mem", "pair")),
        P(("groups", "mem"), "head"),
        P(("groups", "mem"), "head"),
        P(("groups", "mem")),
        P(("groups", "mem")),
    )
    out_specs = P(("groups", "mem", "pair"), "head")
    return jax.shard_map(
        functools.partial(body, mesh.shape["mem"]), mesh=mesh, in_specs=in_specs, out_specs=out_specs,
        check_vma=False,
    )
```

```python
import functools

import jax
import jax.numpy as jnp
from jax import lax
from jax.experimental import pallas as pl
from jax.experimental.pallas import tpu as pltpu
from jax.sharding import PartitionSpec as P

DH = 64
LANES = 256
PACK = LANES // DH
TOP = 16
NEG = -1e30
MESH = pl.DeviceIdType.MESH


def kernel(
    n, rows, groups, slots,
    q_ref, quest_ref, k_hbm, v_hbm, len_ref, pq_ref, out_ref,
    qbuf, obuf, rbuf, stat, rstat, bias, onehot, kbuf, vbuf,
    k_sem, v_sem, qs_sem, qr_sem, os_sem, or_sem, ss_sem, sr_sem,
):
    me = lax.axis_index("mem")
    chunks = groups // 2
    both = 2 * rows
    block = min(n, 4)
    tokens = kbuf.shape[0]
    width = 2 * LANES

    def load(c, hbm, buf, sem):
        cols = pl.ds(pl.multiple_of(c * width, width), width)
        return pltpu.make_async_copy(hbm.at[:, cols], buf.at[:, cols], sem.at[c])

    for c in range(chunks):
        load(c, k_hbm, kbuf, k_sem).start()
        load(c, v_hbm, vbuf, v_sem).start()

    barrier = pltpu.get_barrier_semaphore()
    for k in range(1, n):
        pl.semaphore_signal(barrier, inc=1, device_id={"mem": lax.rem(me + k, n)}, device_id_type=MESH)

    onehot[...] = jnp.zeros_like(onehot)
    ids = lax.broadcasted_iota(jnp.int32, (TOP, rows), 0)
    onehot[:, :rows] = jnp.where(ids == quest_ref[...], 1.0, 0.0)
    qbuf[me, 0:TOP, :] = onehot[...].astype(jnp.bfloat16)
    for c in range(chunks):
        halves = [
            q_ref[:, (2 * c + g) * LANES : (2 * c + g + 1) * LANES].astype(jnp.float32) for g in range(2)
        ]
        qbuf[me, TOP + both * c : TOP + both * (c + 1), :] = jnp.concatenate(halves, 0).astype(jnp.bfloat16)

    pl.semaphore_wait(barrier, n - 1)

    def query_copy(k, c, slot):
        span = pl.ds(0, TOP + both) if c == 0 else pl.ds(TOP + both * c, both)
        return pltpu.make_async_remote_copy(
            src_ref=qbuf.at[slot, span],
            dst_ref=qbuf.at[slot, span],
            send_sem=qs_sem.at[k, c],
            recv_sem=qr_sem.at[k, c],
            device_id={"mem": lax.rem(me + k, n)},
            device_id_type=MESH,
        )

    def relay(c):
        span = pl.ds(0, TOP + both) if c == 0 else pl.ds(TOP + both * c, both)
        place = qbuf.at[lax.rem(me + n - 2, n), span]
        return pltpu.make_async_remote_copy(
            src_ref=place,
            dst_ref=place,
            send_sem=qs_sem.at[0, c],
            recv_sem=qr_sem.at[lax.rem(2 * me - 1 + n, n), c],
            device_id={"mem": lax.rem(3 * (me - 1) + 3 * n, n)},
            device_id_type=MESH,
        )

    def pass_on(c):
        if n == 4:
            query_copy(2, c, lax.rem(me + n - 2, n)).wait_recv()

            @pl.when((me == 1) | (me == 2))
            def _():
                relay(c).start()

    def result_copy(k, c, there, here):
        span = pl.ds(pl.multiple_of(both * c, 16), both)
        return pltpu.make_async_remote_copy(
            src_ref=obuf.at[there, span],
            dst_ref=rbuf.at[here, span],
            send_sem=os_sem.at[k, c],
            recv_sem=or_sem.at[k, c],
            device_id={"mem": lax.rem(me + k, n)},
            device_id_type=MESH,
        )

    def stat_copy(k, there, here):
        return pltpu.make_async_remote_copy(
            src_ref=stat.at[there],
            dst_ref=rstat.at[here],
            send_sem=ss_sem.at[k],
            recv_sem=sr_sem.at[k],
            device_id={"mem": lax.rem(me + k, n)},
            device_id_type=MESH,
        )

    for c in range(chunks):
        for k in [n // 2] + [x for x in range(1, n) if x != n // 2]:
            if n == 4 and k != 2:

                @pl.when(jnp.abs(me - lax.rem(me + k, n)) != 3)
                def _(k=k, c=c):
                    query_copy(k, c, me).start()
            else:
                query_copy(k, c, me).start()

    quest = lax.broadcasted_iota(jnp.int32, (TOP, tokens), 0)
    slot = lax.broadcasted_iota(jnp.int32, (TOP, tokens), 1)
    table = jnp.full((TOP, tokens), NEG, jnp.float32)
    for p in range(tokens // slots):
        good = (slot >= p * slots) & (slot < p * slots + len_ref[p]) & (quest == pq_ref[p])
        table = jnp.where(good, 0.0, table)
    table = table.astype(jnp.bfloat16)
    stat[...] = jnp.zeros_like(stat)

    lane_head = lax.broadcasted_iota(jnp.int32, (1, LANES), 1) // DH
    lane = lax.broadcasted_iota(jnp.int32, (1, 128), 1)

    for c in range(chunks):
        load(c, k_hbm, kbuf, k_sem).wait()
        load(c, v_hbm, vbuf, v_sem).wait()
        if c == 0:
            pass_on(0)
        for k in range(1, n):
            if n != 4 or k != 2:
                query_copy(k, c, lax.rem(me + n - k, n)).wait_recv()

        def some(b, _, c=c):
            if c == 0:
                seen = [
                    jnp.transpose(qbuf[b * block + s, 0:TOP, 0:128].astype(jnp.float32))[:rows]
                    for s in range(block)
                ]
                bias[b] = jnp.dot(
                    jnp.concatenate(seen, 0).astype(jnp.bfloat16), table, preferred_element_type=jnp.float32
                )
            pair = [
                qbuf[b * block + s, TOP + both * c : TOP + both * (c + 1), :].astype(jnp.float32)
                for s in range(block)
            ]
            made = []
            found = [stat[b * block + s] for s in range(block)]
            for g in range(2):
                if g == 1 and n == 4 and c + 1 < chunks:
                    pass_on(c + 1)
                cols = slice((2 * c + g) * LANES, (2 * c + g + 1) * LANES)
                q4 = jnp.concatenate([x[g * rows : (g + 1) * rows] for x in pair], 0)
                spread = jnp.concatenate([jnp.where(lane_head == h, q4, 0.0) for h in range(PACK)], 0)
                scores = lax.dot_general(
                    spread.astype(jnp.bfloat16), kbuf[:, cols], (((1,), (1,)), ((), ())),
                    preferred_element_type=jnp.float32,
                )
                scores = scores.reshape(PACK, block * rows, tokens) + bias[b][None]
                maxima = jnp.max(scores, axis=2, keepdims=True)
                weights = jnp.exp(scores - maxima)
                totals = jnp.sum(weights, axis=2, keepdims=True)
                mixture = jnp.dot(
                    weights.astype(jnp.bfloat16).reshape(PACK * block * rows, tokens), vbuf[:, cols],
                    preferred_element_type=jnp.float32,
                ).reshape(PACK, block * rows, LANES)
                mixture = mixture / totals
                picked = mixture[0]
                for h in range(1, PACK):
                    picked = jnp.where(lane_head == h, mixture[h], picked)
                made.append(picked)
                for h in range(PACK):
                    at = (2 * c + g) * PACK + h
                    for s in range(block):
                        part = slice(s * rows, (s + 1) * rows)
                        found[s] = jnp.where(lane == at, maxima[h, part], found[s])
                        found[s] = jnp.where(lane == 64 + at, totals[h, part], found[s])
            for s in range(block):
                part = slice(s * rows, (s + 1) * rows)
                stat[b * block + s] = found[s]
                obuf[b * block + s, both * c : both * (c + 1), :] = jnp.concatenate(
                    [made[0][part], made[1][part]], 0
                ).astype(jnp.bfloat16)
            return 0

        if n == block:
            some(0, 0)
        else:
            lax.fori_loop(0, n // block, some, 0)
        if c == chunks - 1:
            for k in range(1, n):
                stat_copy(k, lax.rem(me + k, n), me).start()
        for k in [n // 2] + [x for x in range(1, n) if x != n // 2]:
            result_copy(k, c, lax.rem(me + k, n), me).start()

    rstat[me] = stat[me]
    for c in range(chunks):
        span = slice(both * c, both * (c + 1))
        rbuf[me, span, :] = obuf[me, span, :]

    for k in range(1, n):
        stat_copy(k, me, lax.rem(me + n - k, n)).wait_recv()
    top = rstat[0]
    for s in range(1, n):
        top = jnp.maximum(top, rstat[s])
    shares = []
    for s in range(n):
        now = rstat[s]
        shares.append(jnp.exp(now - top) * pltpu.roll(now, 64, 1))
    whole = functools.reduce(lambda a, b: a + b, shares)
    shares = [jnp.where(lane < groups * PACK, x / whole, 0.0) for x in shares]
    shares = jnp.concatenate(shares, 0)
    high = shares.astype(jnp.bfloat16)
    low = (shares - high.astype(jnp.float32)).astype(jnp.bfloat16)
    at_head = lax.broadcasted_iota(jnp.int32, (128, LANES), 0)
    at_lane = lax.broadcasted_iota(jnp.int32, (128, LANES), 1) // DH
    for c in range(chunks):
        for k in range(1, n):
            result_copy(k, c, me, lax.rem(me + n - k, n)).wait_recv()
        factor = []
        for g in range(2):
            expand = jnp.where(at_head == (2 * c + g) * PACK + at_lane, 1.0, 0.0).astype(jnp.bfloat16)
            factor.append(
                jnp.dot(high, expand, preferred_element_type=jnp.float32)
                + jnp.dot(low, expand, preferred_element_type=jnp.float32)
            )
        sums = [0.0, 0.0]
        for s in range(n):
            got = rbuf[s, both * c : both * (c + 1), :].astype(jnp.float32)
            for g in range(2):
                sums[g] = sums[g] + got[g * rows : (g + 1) * rows] * factor[g][s * rows : (s + 1) * rows]
        for g in range(2):
            out_ref[:, (2 * c + g) * LANES : (2 * c + g + 1) * LANES] = sums[g].astype(jnp.bfloat16)

    for k in range(1, n):
        for c in range(chunks):
            if n == 4 and k != 2:

                @pl.when(jnp.abs(me - lax.rem(me + k, n)) != 3)
                def _(k=k, c=c):
                    query_copy(k, c, me).wait_send()

            else:
                query_copy(k, c, me).wait_send()
            if n == 4 and k == 2:

                @pl.when((me == 1) | (me == 2))
                def _(c=c):
                    relay(c).wait_send()

            result_copy(k, c, lax.rem(me + k, n), me).wait_send()
        stat_copy(k, lax.rem(me + k, n), me).wait_send()


def body(n, queries, row_question, keys, values, lengths, passage_question):
    rows, width = queries.shape
    tokens = keys.shape[0]
    groups = width // LANES
    chunks = groups // 2
    block = min(n, 4)
    bf16, f32 = jnp.bfloat16, jnp.float32
    vmem = pl.BlockSpec(memory_space=pltpu.VMEM)
    smem = pl.BlockSpec(memory_space=pltpu.SMEM)
    anywhere = pl.BlockSpec(memory_space=pl.ANY)
    return pl.pallas_call(
        functools.partial(kernel, n, rows, groups, tokens // lengths.shape[0]),
        out_shape=jax.ShapeDtypeStruct((rows, width), bf16),
        in_specs=[vmem, vmem, anywhere, anywhere, smem, smem],
        out_specs=vmem,
        scratch_shapes=[
            pltpu.VMEM((n, TOP + groups * rows, LANES), bf16),
            pltpu.VMEM((n, groups * rows, LANES), bf16),
            pltpu.VMEM((n, groups * rows, LANES), bf16),
            pltpu.VMEM((n, rows, 128), f32),
            pltpu.VMEM((n, rows, 128), f32),
            pltpu.VMEM((n // block, block * rows, tokens), f32),
            pltpu.VMEM((TOP, LANES), f32),
            pltpu.VMEM((tokens, width), bf16),
            pltpu.VMEM((tokens, width), bf16),
            pltpu.SemaphoreType.DMA((chunks,)),
            pltpu.SemaphoreType.DMA((chunks,)),
            pltpu.SemaphoreType.DMA((n, chunks)),
            pltpu.SemaphoreType.DMA((n, chunks)),
            pltpu.SemaphoreType.DMA((n, chunks)),
            pltpu.SemaphoreType.DMA((n, chunks)),
            pltpu.SemaphoreType.DMA((n,)),
            pltpu.SemaphoreType.DMA((n,)),
        ],
        compiler_params=pltpu.CompilerParams(
            collective_id=0, has_side_effects=True, vmem_limit_bytes=60 * 1024 * 1024
        ),
        cost_estimate=pl.CostEstimate(
            flops=4 * n * rows * width * tokens,
            bytes_accessed=4 * tokens * width,
            transcendentals=n * rows * tokens * (width // DH),
        ),
    )(queries, row_question.reshape(1, rows), keys, values, lengths, passage_question)


def solution(mesh):
    in_specs = (
        P(("groups", "mem", "pair"), "head"),
        P(("groups", "mem", "pair")),
        P(("groups", "mem"), "head"),
        P(("groups", "mem"), "head"),
        P(("groups", "mem")),
        P(("groups", "mem")),
    )
    out_specs = P(("groups", "mem", "pair"), "head")
    return jax.shard_map(
        functools.partial(body, mesh.shape["mem"]), mesh=mesh, in_specs=in_specs, out_specs=out_specs,
        check_vma=False,
    )
```
